32 devices in a mesh: groups: 1, expert: 32 (over z, y, x, core).
Axes of the slice: x: 2, y: 2, z: 4, core: 2. Of those that a mesh axis runs over, the one named last changes fastest.
Arguments:
- tokens: bfloat16 [512, 8192], P(('groups', 'expert')), may hold values from -6 to 6
- gate_up: bfloat16 [32, 4096, 512], P(('groups', 'expert')), may hold values from -0.0625 to 0.0625
- down_proj: bfloat16 [32, 256, 4096], P(('groups', 'expert')), may hold values from -0.375 to 0.375
- expert_ids: int32 [512, 8], P(('groups', 'expert')), may hold values from 0 to 15, all different within a row; in each aligned block of 16 rows (0 to 15, 16 to 31, ...) at most 10 rows name the same one
- combine: float32 [512, 8], P(('groups', 'expert')), may hold values from 0.05 to 0.3
- teacher: bfloat16 [512, 8192], P(('groups', 'expert')), may hold values from -4 to 4
Outputs:
- student: bfloat16 [512, 8192], P(('groups', 'expert'))
- down_grad: bfloat16 [32, 256, 4096], P(('groups', 'expert'))
The draws below stay inside these ranges and needn't reach their ends.
Inputs may be any that keep to these rules, and one draw needn't show every extreme that they name: `expert_ids`: each row names 8 different experts; within the rows of one device no expert is named by more than 10 rows, a bound that some block reaches.
All inputs are finite; a program needn't handle non-finite values.
Results may differ from the reference program's by a relative error of at most 0.0072.
Values may be sent and summed in bfloat16 or wider, within the bound.
A program may use at most 64 MiB of HBM per device.

```python
import math
import jax
import jax.numpy as jnp
import numpy as np
from jax import lax

D = 8192
U = 256
TOP = 8
TOK_DEV = 16
EXPERTS = 16
HALVES = 32
TOKENS = 512
CAP = 10
N_EXPERT = 32


def levels(own_key, extent, cuts, low, largest):
    def one(axis_at, parts):
        draws = jax.random.uniform(jax.random.fold_in(jax.random.fold_in(own_key, 6), axis_at), (parts,), jnp.float32, low / len(cuts), largest / len(cuts))
        return jnp.repeat(jnp.exp(draws), extent[axis_at] // parts).reshape((-1,) + (1,) * (len(extent) - axis_at - 1))

    loudness = one(*cuts[0])
    for cut in cuts[1:]:
        loudness = loudness * one(*cut)
    return loudness


def shared_out(stream_key, own, number, rows, count, top, bound, slope):
    ranking = jax.random.permutation(stream_key, count)
    packed, common = shares(count, rows * top, bound, slope, True), shares(count, rows * top, bound, slope, False)
    places = jnp.arange(count)

    def named(sizes, offset_by):
        used = int((sizes > 0).sum())
        fixed = max(1, used // 4)
        passed = fixed + (places - fixed + offset_by * (used - fixed)) % max(1, count - fixed)
        return jnp.zeros((count,), jnp.int32).at[ranking[jnp.where(places < fixed, places, passed)]].set(jnp.asarray(sizes, jnp.int32))

    sizes = jnp.where(number % 4 == 0, named(packed, number // 4), named(common, number - number // 4 - 1))
    mixed = jax.random.permutation(jax.random.fold_in(own, 3), count)
    donor, sink = mixed[0:count // 2 * 2:2], mixed[1:count // 2 * 2:2]
    room = jnp.minimum(sizes[donor] - 1, bound - sizes[sink]) // 2
    room = jnp.where((donor == ranking[0]) | (sink == ranking[0]) | (sizes[sink] == 0), 0, jnp.maximum(room, 0))
    passed = jax.random.randint(jax.random.fold_in(own, 4), (count // 2,), 0, 1 << 20) % (room + 1)
    sizes = sizes.at[donor].add(-passed).at[sink].add(passed)
    items = jnp.searchsorted(jnp.cumsum(sizes), jnp.arange(rows * top), side="right").astype(jnp.int32)
    table = items.reshape(top, rows).T
    table = table[jax.random.permutation(jax.random.fold_in(own, 1), rows)]
    offset_by = jax.random.randint(jax.random.fold_in(own, 2), (rows, 1), 0, top)
    return jnp.take_along_axis(table, (jnp.arange(top)[None, :] + offset_by) % top, axis=1)


def shares(number_of, total, reach, slope, full):
    weights = [(1 << 20) // math.isqrt(rank ** slope) + 1 for rank in range(1, number_of + 1)]
    largest = reach if full else min(reach, max(-(-total // number_of), total * weights[0] // sum(weights)))
    least = 1 if total - largest >= number_of - 1 else 0
    given, surplus = [largest] + [least] * (number_of - 1), total - largest - least * (number_of - 1)
    while surplus > 0:
        movable = [i for i in range(1, number_of) if given[i] < largest] or [i for i in range(1, number_of) if given[i] < reach]
        pool, left = sum([weights[i] for i in movable]), surplus
        for i in movable:
            extra = min(reach - given[i], max(1, left * weights[i] // pool), surplus)
            given[i] = given[i] + extra
            surplus = surplus - extra
    return np.array(given)


def gaussian(stream_key, shape, width, limit, cuts=(), kind=jnp.bfloat16):
    entries = jax.random.normal(stream_key, shape, jnp.float32) * width
    if len(cuts) > 0:
        entries = levels(stream_key, shape, cuts, -0.22, 0.18) * entries
    return jnp.clip(entries, min=-limit, max=limit).astype(kind)


def setup_inputs(seed: int = 0, part: int = 0) -> dict:
    arg_keys = jax.random.split(jax.random.key(seed), 7)
    part_keys = jax.random.split(jax.random.fold_in(arg_keys[6], part), 7)
    tokens = gaussian(part_keys[0], (TOKENS, D), 1.0, 6.0, ((0, 32),))
    gate_up = gaussian(part_keys[1], (HALVES, D // 2, 2 * U), D ** -0.5, 0.0625, ((0, 32),))
    down_proj = gaussian(part_keys[2], (HALVES, U, D // 2), U ** -0.5, 0.375, ((0, 32),))
    expert_ids_keys = jax.random.split(jax.random.fold_in(part_keys[3], 1), TOKENS // TOK_DEV)
    expert_ids_turns = jax.random.permutation(jax.random.fold_in(part_keys[3], 3), TOKENS // TOK_DEV)
    expert_ids = jax.vmap(lambda own, number: shared_out(jax.random.fold_in(part_keys[3], 2), own, number, TOK_DEV, EXPERTS, TOP, CAP, 2))(expert_ids_keys, expert_ids_turns).reshape((TOKENS, TOP))
    combine = jnp.clip(0.05 + 0.25 * jax.random.uniform(part_keys[4], (TOKENS, TOP), jnp.float32) ** levels(part_keys[4], (TOKENS, TOP), ((0, 32),), -0.2, 0.2), 0.05, 0.3)
    teacher = gaussian(part_keys[5], (TOKENS, D), 0.5, 4.0, ((0, 32),))
    return dict(tokens=tokens, gate_up=gate_up, down_proj=down_proj, expert_ids=expert_ids, combine=combine, teacher=teacher)


def slot_plan(block_ids):
    flat_expert = block_ids.reshape(-1).astype(jnp.int32)
    onehot = (flat_expert[:, None] == jnp.arange(EXPERTS, dtype=jnp.int32)[None, :]).astype(jnp.int32)
    before = jnp.cumsum(onehot, axis=0) - onehot
    position = jnp.sum(before * onehot, axis=1).astype(jnp.int32)
    return flat_expert, position


def reference(tokens, gate_up, down_proj, expert_ids, combine, teacher):
    pair_count = TOK_DEV * TOP
    per_expert = N_EXPERT * CAP
    flat_expert, position = jax.vmap(slot_plan)(expert_ids.reshape(N_EXPERT, TOK_DEV, TOP))
    source = jnp.arange(N_EXPERT, dtype=jnp.int32)[:, None]
    pair_index = source * pair_count + jnp.arange(pair_count, dtype=jnp.int32)[None, :]
    slot_index = flat_expert * per_expert + source * CAP + position
    slot_pair = jnp.full((EXPERTS * per_expert,), TOKENS * TOP, jnp.int32)
    slot_pair = slot_pair.at[slot_index.reshape(-1)].set(pair_index.reshape(-1)).reshape(EXPERTS, per_expert)
    slot_row = jnp.where(slot_pair < TOKENS * TOP, slot_pair // TOP, TOKENS).astype(jnp.int32)
    w_first = gate_up.reshape(EXPERTS, D, 2 * U)
    w_second = down_proj.reshape(EXPERTS, 2, U, D // 2).transpose(0, 2, 1, 3).reshape(EXPERTS, U, D)
    weight_flat = combine.reshape(-1)

    def forward(student, inputs):
        rows, pairs_of, first, second = inputs
        rows_in = jnp.take(tokens, rows, axis=0, mode="fill", fill_value=0)
        pre_act = jnp.dot(rows_in, first, preferred_element_type=jnp.float32)
        hidden = (jax.nn.silu(pre_act[:, :U]) * pre_act[:, U:]).astype(jnp.bfloat16)
        outputs = jnp.dot(hidden, second, preferred_element_type=jnp.float32).astype(jnp.bfloat16)
        weights = jnp.take(weight_flat, pairs_of, mode="fill", fill_value=0)
        student = student.at[rows].add(weights[:, None] * outputs.astype(jnp.float32), mode="drop")
        return student, hidden

    student, hidden_all = lax.scan(forward, jnp.zeros((TOKENS, D), jnp.float32), (slot_row, slot_pair, w_first, w_second))
    student_out = student.astype(jnp.bfloat16)
    error_rows = student_out.astype(jnp.float32) - teacher.astype(jnp.float32)

    def backward(inputs):
        rows, pairs_of, hidden = inputs
        weights = jnp.take(weight_flat, pairs_of, mode="fill", fill_value=0)
        picked = jnp.take(error_rows, rows, axis=0, mode="fill", fill_value=0)
        scaled = (weights[:, None] * picked).astype(jnp.bfloat16)
        gradient = jnp.dot(hidden.T, scaled, preferred_element_type=jnp.float32).astype(jnp.bfloat16)
        return gradient.reshape(U, 2, D // 2).transpose(1, 0, 2)

    gradients = lax.map(backward, (slot_row, slot_pair, hidden_all))
    return student_out, gradients.reshape(N_EXPERT, U, D // 2)
```

```python
import jax
import jax.numpy as jnp
from jax import lax
from jax.sharding import PartitionSpec as P


def swap_cores(block):
    count = lax.axis_size("expert")
    return lax.ppermute(block, "expert", [(i, i ^ 1) for i in range(count)])


def dense_weights(expert_ids, combine, experts):
    match = expert_ids[:, :, None] == jnp.arange(experts, dtype=jnp.int32)[None, None, :]
    return jnp.sum(jnp.where(match, combine[:, :, None], 0.0), axis=1)


def shards(tokens, gate_up, down_proj, expert_ids, combine, teacher):
    row_count, width = tokens.shape
    count = lax.axis_size("expert")
    experts = count // 2
    unit_count = down_proj.shape[1]
    half = width // 2
    me = lax.axis_index("expert")
    expert, core = me // 2, me % 2
    same_core = [list(range(0, count, 2)), list(range(1, count, 2))]

    def chip_rows(rows):
        kept = lax.dynamic_slice(rows, (0, core * half), (row_count, half))
        given = lax.dynamic_slice(rows, (0, (1 - core) * half), (row_count, half))
        got = swap_cores(given)
        first = jnp.where(core == 0, kept, got)
        second = jnp.where(core == 0, got, kept)
        return jnp.concatenate([first, second], axis=0)

    def gather(block):
        return lax.all_gather(block, "expert", axis_index_groups=same_core, axis=0, tiled=True)

    weights = lax.all_gather(dense_weights(expert_ids, combine, experts), "expert", axis=0, tiled=True)
    weight = lax.dynamic_slice(weights, (0, expert), (weights.shape[0], 1))
    taught = chip_rows(teacher)
    rows_in = gather(chip_rows(tokens))
    partial = jnp.dot(rows_in, gate_up[0], preferred_element_type=jnp.float32)
    pre = partial + swap_cores(partial)
    hidden = jax.nn.silu(pre[:, :unit_count]) * pre[:, unit_count:]
    weighed = (weight * hidden).astype(jnp.bfloat16)
    part = jnp.dot(weighed, down_proj[0], preferred_element_type=jnp.float32).astype(jnp.bfloat16)
    block = lax.psum_scatter(part, "expert", axis_index_groups=same_core, scatter_dimension=0, tiled=True)
    error = (block.astype(jnp.float32) - taught.astype(jnp.float32)).astype(jnp.bfloat16)
    mine = lax.dynamic_slice(block, (core * row_count, 0), (row_count, half))
    theirs = swap_cores(lax.dynamic_slice(block, ((1 - core) * row_count, 0), (row_count, half)))
    student = jnp.concatenate(
        [jnp.where(core == 0, mine, theirs), jnp.where(core == 0, theirs, mine)], axis=1
    )
    errors = gather(error)
    gradient = jnp.einsum("su,sd->ud", weighed, errors, preferred_element_type=jnp.float32)
    return (student, gradient.astype(jnp.bfloat16).reshape(1, unit_count, half))


def solution(mesh):
    in_specs = (
        P(("groups", "expert"), None),
        P(("groups", "expert"), None, None),
        P(("groups", "expert"), None, None),
        P(("groups", "expert"), None),
        P(("groups", "expert"), None),
        P(("groups", "expert"), None),
    )
    out_specs = (P(("groups", "expert"), None), P(("groups", "expert"), None, None))
    return jax.shard_map(shards, mesh=mesh, in_specs=in_specs, out_specs=out_specs, check_vma=False)
```

```python
import functools

import jax
import jax.numpy as jnp
from jax import lax
from jax.experimental import pallas as pl
from jax.experimental.pallas import tpu as pltpu
from jax.sharding import PartitionSpec as P

MESH = pl.DeviceIdType.MESH
RING, LINE, TAIL, TILE = 4, 4, 128, 512
GATHER_ORDER = ((0, 1, 2, 3), (1, 2, 0, 3), (2, 1, 3, 0), (3, 2, 1, 0))
REDUCE_ORDER = ((2, 3, 1, 0), (2, 3, 0, 1), (1, 0, 3, 2), (1, 0, 2, 3))


def kernel(
    tokens, gate_up, down_proj, ids, combine, teacher, student_out, grad_out,
    tok, gate, down, taught, own_pre, got_pre, hidden_t, part, part_a, part_b,
    part_l, part_r, line_up, line_down, student, errors, total, grad, sem,
):
    rows = ids.shape[0]
    block, plane = 2 * rows, RING * 2 * rows
    half = down.shape[1]
    unit_count = down.shape[0]
    experts = RING * LINE
    me = lax.axis_index("expert")
    core, chip = me % 2, me // 2
    z, y, x = chip // 4, (chip // 2) % 2, chip % 2
    p = y * 2 + (x + y) % 2

    def device(at_z, q):
        at_y = q // 2
        at_x = (q % 2 + at_y) % 2
        return ((at_z * 2 + at_y) * 2 + at_x) * 2 + core

    partner = me + 1 - 2 * core
    after, before, across = (p + 1) % 4, (p + 3) % 4, (p + 2) % 4
    right, left = device(z, after), device(z, before)
    above, below = device((z + 1) % LINE, p), device((z + LINE - 1) % LINE, p)
    not_top, not_bottom = z < LINE - 1, z > 0
    power = (1 + 3 * (z % 2)) * (1 + 15 * (z // 2))

    def order(table, k):
        packed = sum(table[i][k] * LINE**i for i in range(LINE))
        return (packed // power) % LINE

    names = {}

    def flag(name, at=0):
        base = names.setdefault(name, len(names))
        return sem.at[base * LINE + at]

    pending = []

    def always(body):
        body()

    def send(source, target, name, at, to, condition=None):
        copy = pltpu.make_async_remote_copy(
            src_ref=source, dst_ref=target, send_sem=flag(name + "s", at),
            recv_sem=flag(name + "r", at), device_id={"expert": to}, device_id_type=MESH,
        )
        when = always if condition is None else pl.when(condition)

        @when
        def _():
            copy.start()

        pending.append((when, copy))

    def arrived(target, name, at=0):
        pltpu.make_async_remote_copy(
            src_ref=target, dst_ref=target, send_sem=flag(name + "s", at),
            recv_sem=flag(name + "r", at), device_id={"expert": partner}, device_id_type=MESH,
        ).wait_recv()

    def local(source, target, name):
        copy = pltpu.make_async_copy(source, target, flag(name))
        copy.start()
        return copy

    def span(at_z, q):
        return pl.ds(pl.multiple_of((at_z * RING + q) * block, block), block)

    def part_span(at_z, q, side):
        return pl.ds(pl.multiple_of((at_z * RING + q) * block + side * rows, rows), rows)

    def plane_span(at_z):
        return pl.ds(pl.multiple_of(at_z * plane, plane), plane)

    kept = pl.ds(pl.multiple_of(core * half, half), half)
    given = pl.ds(pl.multiple_of((1 - core) * half, half), half)
    my_rows = part_span(z, p, core)
    its_rows = part_span(z, p, 1 - core)
    front, tail = pl.ds(0, half), pl.ds(half, TAIL)
    core_rows = pl.ds(pl.multiple_of(core * rows, rows), rows)
    other_rows = pl.ds(pl.multiple_of((1 - core) * rows, rows), rows)

    tok_load = local(tokens.at[:, kept], tok.at[my_rows, front], "tok")
    gate_load = local(gate_up.at[0], gate, "gate")
    down_load = local(down_proj.at[0], down, "down")
    taught_load = local(teacher.at[:, kept], taught.at[core_rows, :], "taught")

    barrier = pltpu.get_barrier_semaphore()
    for to in (partner, right, left):
        pl.semaphore_signal(barrier, inc=1, device_id={"expert": to}, device_id_type=MESH)

    @pl.when(not_top)
    def _():
        pl.semaphore_signal(barrier, inc=1, device_id={"expert": above}, device_id_type=MESH)

    @pl.when(not_bottom)
    def _():
        pl.semaphore_signal(barrier, inc=1, device_id={"expert": below}, device_id_type=MESH)

    lane = lax.broadcasted_iota(jnp.int32, (rows, TAIL), 1)
    weight = jnp.zeros((rows, TAIL), jnp.float32)
    for k in range(ids.shape[1]):
        weight += jnp.where(ids[:, k : k + 1] == lax.rem(lane, experts), combine[:, k : k + 1], 0.0)
    high = weight.astype(jnp.bfloat16).astype(jnp.float32)
    middle = (weight - high).astype(jnp.bfloat16).astype(jnp.float32)
    low = weight - high - middle
    coded = jnp.where(lane < experts, high, jnp.where(lane < 2 * experts, middle, low))
    coded = jnp.where(lane < 3 * experts, coded, 0.0)
    tok[my_rows, tail] = coded.astype(jnp.bfloat16)

    pl.semaphore_wait(barrier, 3 + (LINE - 1 - z + LINE - 2) // (LINE - 1) + (z + LINE - 2) // (LINE - 1))

    send(tokens.at[:, given], tok.at[my_rows, front], "tokx", 0, partner)
    send(tok.at[my_rows, tail], tok.at[my_rows, tail], "tailx", 0, partner)
    send(teacher.at[:, given], taught.at[core_rows, :], "taughtx", 0, partner)
    tok_load.wait()
    arrived(tok.at[its_rows, front], "tokx")
    arrived(tok.at[its_rows, tail], "tailx")

    def start(buffer, tag, k):
        at_z = order(GATHER_ORDER, k)
        here = buffer.at[span(at_z, p)]
        if k > 0:
            arrived(here, tag + "z", at_z)
        send(here, here, tag + "z", at_z, above, (at_z <= z) & not_top)
        copy = pltpu.make_async_remote_copy(
            src_ref=here, dst_ref=here, send_sem=flag(tag + "d", at_z),
            recv_sem=flag(tag + "zr", at_z), device_id={"expert": below}, device_id_type=MESH,
        )
        when = pl.when((at_z >= z) & not_bottom)

        @when
        def _():
            copy.start()

        pending.append((when, copy))
        send(here, here, tag + "l", at_z, right)
        send(here, here, tag + "r", at_z, left)

    def forward(buffer, tag, k):
        at_z = order(GATHER_ORDER, k)
        arrived(buffer.at[span(at_z, before)], tag + "l", at_z)
        piece = buffer.at[part_span(at_z, before, 0)]
        send(piece, piece, tag + "ol", at_z, right)
        arrived(buffer.at[span(at_z, after)], tag + "r", at_z)
        piece = buffer.at[part_span(at_z, after, 1)]
        send(piece, piece, tag + "or", at_z, left)

    def complete(buffer, tag, k):
        at_z = order(GATHER_ORDER, k)
        arrived(buffer.at[part_span(at_z, across, 0)], tag + "ol", at_z)
        arrived(buffer.at[part_span(at_z, across, 1)], tag + "or", at_z)

    def gathered(buffer, tag, visit):
        start(buffer, tag, 0)
        start(buffer, tag, 1)
        forward(buffer, tag, 0)
        start(buffer, tag, 2)
        forward(buffer, tag, 1)
        complete(buffer, tag, 0)
        visit(0)
        start(buffer, tag, 3)
        forward(buffer, tag, 2)
        complete(buffer, tag, 1)
        visit(1)
        forward(buffer, tag, 3)
        complete(buffer, tag, 2)
        visit(2)
        complete(buffer, tag, 3)
        visit(3)

    def multiply(k):
        at_z = order(GATHER_ORDER, k)
        own_pre[k] = jnp.dot(
            tok[plane_span(at_z), front], gate[...], preferred_element_type=jnp.float32
        )
        send(own_pre.at[k], got_pre.at[k], "pre", k, partner)

    def finish(k):
        at_z = order(GATHER_ORDER, k)
        arrived(got_pre.at[k], "pre", k)
        pre = own_pre[k] + got_pre[k]
        gated, up = pre[:, :unit_count], pre[:, unit_count:]
        lanes = lax.broadcasted_iota(jnp.int32, (plane, TAIL), 1)
        mine = (lax.rem(lanes, experts) == chip) & (lanes < 3 * experts)
        coded = tok[plane_span(at_z), tail].astype(jnp.float32)
        share = jnp.sum(jnp.where(mine, coded, 0.0), axis=1, keepdims=True)
        hidden = gated / (1.0 + jnp.exp(-gated)) * up * share
        hidden_t[at_z] = hidden.T.astype(jnp.bfloat16)
        lowered = hidden.astype(jnp.bfloat16)

        @pl.loop(0, half // TILE)
        def _(t):
            columns = pl.ds(pl.multiple_of(t * TILE, TILE), TILE)
            part[plane_span(at_z), columns] = jnp.dot(
                lowered, down[:, columns], preferred_element_type=jnp.float32
            ).astype(jnp.bfloat16)

    def send_first(k):
        at_z = order(REDUCE_ORDER, k)
        send(part.at[part_span(at_z, across, 0)], part_a.at[at_z], "a", at_z, right)
        send(part.at[part_span(at_z, across, 1)], part_b.at[at_z], "b", at_z, left)
        send(part.at[part_span(at_z, after, 1)], part_l.at[at_z, 1], "l1", at_z, right)
        send(part.at[part_span(at_z, before, 0)], part_r.at[at_z, 0], "r0", at_z, left)

    def add_up(target, *terms):
        @pl.loop(0, half // TILE)
        def _(t):
            columns = pl.ds(pl.multiple_of(t * TILE, TILE), TILE)
            value = terms[0](columns).astype(jnp.float32)
            for term in terms[1:]:
                value += term(columns).astype(jnp.float32)
            target(columns, value)

    def send_second(k):
        at_z = order(REDUCE_ORDER, k)
        for name, got, q, side, to in (
            ("a", part_a, after, 0, right), ("b", part_b, before, 1, left)
        ):
            arrived(got.at[at_z], name, at_z)
            piece = part_span(at_z, q, side)

            def put(columns, value, piece=piece):
                part[piece, columns] = value.astype(jnp.bfloat16)

            add_up(put, lambda c, piece=piece: part[piece, c], lambda c, got=got: got[at_z, :, c])
            if side == 0:
                send(part.at[piece], part_l.at[at_z, 0], "l0", at_z, to)
            else:
                send(part.at[piece], part_r.at[at_z, 1], "r1", at_z, to)

    def reduce_line(k):
        at_z = order(REDUCE_ORDER, k)
        for side in range(2):
            arrived(part_l.at[at_z, side], "l%d" % side, at_z)
            arrived(part_r.at[at_z, side], "r%d" % side, at_z)

        def summed(put, *more):
            for side in range(2):
                piece = part_span(at_z, p, side)
                add_up(
                    functools.partial(put, side),
                    lambda c: part[piece, c],
                    lambda c: part_l[at_z, side, :, c],
                    lambda c: part_r[at_z, side, :, c],
                    *[lambda c, ref=ref: ref[at_z, pl.ds(side * rows, rows), c] for ref in more],
                )

        if k < LINE - 1:
            def put(side, columns, value):
                part[part_span(at_z, p, side), columns] = value.astype(jnp.bfloat16)
        else:
            def put(side, columns, value):
                inner = pl.ds(side * rows, rows)
                rounded = value.astype(jnp.bfloat16)
                student[inner, columns] = rounded
                error = rounded.astype(jnp.float32) - taught[inner, columns].astype(jnp.float32)
                errors[part_span(at_z, p, side), columns] = error.astype(jnp.bfloat16)

        if k < LINE - 1:
            from_below, from_above = (at_z > z) & not_bottom, (at_z < z) & not_top

            @pl.when(from_below)
            def _():
                arrived(line_up.at[at_z], "u", at_z)
                summed(put, line_up)

            @pl.when(from_above)
            def _():
                arrived(line_down.at[at_z], "d", at_z)
                summed(put, line_down)

            @pl.when(((at_z > z) & (z == 0)) | ((at_z < z) & (z == LINE - 1)))
            def _():
                summed(put)

            mine = part.at[span(at_z, p)]
            send(mine, line_up.at[at_z], "u", at_z, above, at_z > z)
            send(mine, line_down.at[at_z], "d", at_z, below, at_z < z)
        else:
            @pl.when(z == 0)
            def _():
                arrived(line_down.at[at_z], "d", at_z)
                summed(put, line_down)

            @pl.when(z == LINE - 1)
            def _():
                arrived(line_up.at[at_z], "u", at_z)
                summed(put, line_up)

            @pl.when(not_top & not_bottom)
            def _():
                arrived(line_up.at[at_z], "u", at_z)
                arrived(line_down.at[at_z], "d", at_z)
                summed(put, line_up, line_down)

    def forward_visit(k):
        if k == 0:
            gate_load.wait()
        multiply(k)
        if k == 1:
            down_load.wait()
        if k in (1, 2):
            finish(k - 1)
        if k in (2, 3):
            finish(k)
        if k == 2:
            send_first(0)

    gathered(tok, "t", forward_visit)
    send_first(1)
    send_second(0)
    send_first(2)
    send_second(1)
    reduce_line(0)
    send_first(3)
    send_second(2)
    reduce_line(1)
    send_second(3)
    reduce_line(2)
    taught_load.wait()
    arrived(taught.at[other_rows, :], "taughtx")
    reduce_line(3)

    stores = [local(student.at[core_rows, :], student_out.at[:, kept], "student")]

    def backward_visit(k):
        at_z = order(GATHER_ORDER, k)
        if k == 0:
            send(student.at[other_rows, :], student_out.at[:, kept], "studentx", 0, partner)

        @pl.loop(0, half // TILE)
        def _(t):
            columns = pl.ds(pl.multiple_of(t * TILE, TILE), TILE)
            value = jnp.dot(
                hidden_t[at_z], errors[plane_span(at_z), columns], preferred_element_type=jnp.float32
            )
            if k > 0:
                value += total[:, columns]
            if k < LINE - 1:
                total[:, columns] = value
            else:
                grad[:, columns] = value.astype(jnp.bfloat16)

    gathered(errors, "e", backward_visit)
    stores.append(local(grad, grad_out.at[0], "grad"))
    for copy in stores:
        copy.wait()
    arrived(student_out.at[:, given], "studentx")
    for when, copy in pending:
        @when
        def _(copy=copy):
            copy.wait_send()


def fused(tokens, gate_up, down_proj, expert_ids, combine, teacher):
    rows, width = tokens.shape
    half = width // 2
    unit_count = down_proj.shape[1]
    all_rows, block = RING * LINE * 2 * rows, 2 * rows
    plane = RING * block
    anywhere, vmem = pl.BlockSpec(memory_space=pl.ANY), pl.BlockSpec(memory_space=pltpu.VMEM)
    low, full = jnp.bfloat16, jnp.float32
    return pl.pallas_call(
        kernel,
        out_shape=(
            jax.ShapeDtypeStruct((rows, width), low),
            jax.ShapeDtypeStruct((1, unit_count, half), low),
        ),
        in_specs=[anywhere, anywhere, anywhere, vmem, vmem, anywhere],
        out_specs=(anywhere, anywhere),
        scratch_shapes=[
            pltpu.VMEM((all_rows, half + TAIL), low),
            pltpu.VMEM((half, 2 * unit_count), low),
            pltpu.VMEM((unit_count, half), low),
            pltpu.VMEM((block, half), low),
            pltpu.VMEM((LINE, plane, 2 * unit_count), full),
            pltpu.VMEM((LINE, plane, 2 * unit_count), full),
            pltpu.VMEM((LINE, unit_count, plane), low),
            pltpu.VMEM((all_rows, half), low),
            pltpu.VMEM((LINE, rows, half), low),
            pltpu.VMEM((LINE, rows, half), low),
            pltpu.VMEM((LINE, 2, rows, half), low),
            pltpu.VMEM((LINE, 2, rows, half), low),
            pltpu.VMEM((LINE, block, half), low),
            pltpu.VMEM((LINE, block, half), low),
            pltpu.VMEM((block, half), low),
            pltpu.VMEM((all_rows, half), low),
            pltpu.VMEM((unit_count, half), full),
            pltpu.VMEM((unit_count, half), low),
            pltpu.SemaphoreType.DMA((64 * LINE,)),
        ],
        compiler_params=pltpu.CompilerParams(
            collective_id=0, has_side_effects=True, vmem_limit_bytes=56 * 2**20
        ),
        cost_estimate=pl.CostEstimate(flops=5 * 10**9, bytes_accessed=10**7, transcendentals=10**5),
    )(tokens, gate_up, down_proj, expert_ids, combine, teacher)


def swap_cores(block):
    count = lax.axis_size("expert")
    return lax.ppermute(block, "expert", [(i, i ^ 1) for i in range(count)])


def dense_weights(expert_ids, combine, experts):
    match = expert_ids[:, :, None] == jnp.arange(experts, dtype=jnp.int32)[None, None, :]
    return jnp.sum(jnp.where(match, combine[:, :, None], 0.0), axis=1)


def spread(tokens, gate_up, down_proj, expert_ids, combine, teacher):
    row_count, width = tokens.shape
    count = lax.axis_size("expert")
    experts = count // 2
    unit_count = down_proj.shape[1]
    half = width // 2
    me = lax.axis_index("expert")
    expert, core = me // 2, me % 2
    same_core = [list(range(0, count, 2)), list(range(1, count, 2))]

    def chip_rows(rows):
        kept = lax.dynamic_slice(rows, (0, core * half), (row_count, half))
        given = lax.dynamic_slice(rows, (0, (1 - core) * half), (row_count, half))
        got = swap_cores(given)
        first = jnp.where(core == 0, kept, got)
        second = jnp.where(core == 0, got, kept)
        return jnp.concatenate([first, second], axis=0)

    def gather(block):
        return lax.all_gather(block, "expert", axis_index_groups=same_core, axis=0, tiled=True)

    weights = lax.all_gather(dense_weights(expert_ids, combine, experts), "expert", axis=0, tiled=True)
    weight = lax.dynamic_slice(weights, (0, expert), (weights.shape[0], 1))
    taught = chip_rows(teacher)
    rows_in = gather(chip_rows(tokens))
    partial = jnp.dot(rows_in, gate_up[0], preferred_element_type=jnp.float32)
    pre = partial + swap_cores(partial)
    hidden = jax.nn.silu(pre[:, :unit_count]) * pre[:, unit_count:]
    weighed = (weight * hidden).astype(jnp.bfloat16)
    part = jnp.dot(weighed, down_proj[0], preferred_element_type=jnp.float32).astype(jnp.bfloat16)
    block = lax.psum_scatter(part, "expert", axis_index_groups=same_core, scatter_dimension=0, tiled=True)
    error = (block.astype(jnp.float32) - taught.astype(jnp.float32)).astype(jnp.bfloat16)
    mine = lax.dynamic_slice(block, (core * row_count, 0), (row_count, half))
    theirs = swap_cores(lax.dynamic_slice(block, ((1 - core) * row_count, 0), (row_count, half)))
    student = jnp.concatenate(
        [jnp.where(core == 0, mine, theirs), jnp.where(core == 0, theirs, mine)], axis=1
    )
    errors = gather(error)
    gradient = jnp.einsum("su,sd->ud", weighed, errors, preferred_element_type=jnp.float32)
    return (student, gradient.astype(jnp.bfloat16).reshape(1, unit_count, half))


def solution(mesh):
    in_specs = (
        P(("groups", "expert"), None),
        P(("groups", "expert"), None, None),
        P(("groups", "expert"), None, None),
        P(("groups", "expert"), None),
        P(("groups", "expert"), None),
        P(("groups", "expert"), None),
    )
    out_specs = (P(("groups", "expert"), None), P(("groups", "expert"), None, None))
    small = mesh.shape["expert"] == 2 * RING * LINE
    shards = fused if small else spread
    return jax.shard_map(shards, mesh=mesh, in_specs=in_specs, out_specs=out_specs, check_vma=False)
```

```python
import functools

import jax
import jax.numpy as jnp
from jax import lax
from jax.experimental import pallas as pl
from jax.experimental.pallas import tpu as pltpu
from jax.sharding import PartitionSpec as P

MESH = pl.DeviceIdType.MESH
RING, LINE, TAIL, TILE = 4, 4, 128, 512
GATHER_ORDER = ((0, 1, 2, 3), (1, 2, 0, 3), (2, 1, 3, 0), (3, 2, 1, 0))
REDUCE_ORDER = ((2, 3, 1, 0), (2, 3, 0, 1), (1, 0, 3, 2), (1, 0, 2, 3))


def kernel(
    tokens, gate_up, down_proj, ids, combine, teacher, student_out, grad_out,
    tok, gate, down, taught, own_pre, got_pre, hidden_t, part, part_a, part_b,
    part_l, part_r, line_up, line_down, student, errors, total, grad, sem,
):
    rows = tokens.shape[0]
    block, plane = 2 * rows, RING * 2 * rows
    half = down.shape[1]
    unit_count = down.shape[0]
    experts = RING * LINE
    me = lax.axis_index("expert")
    core, chip = me % 2, me // 2
    z, y, x = chip // 4, (chip // 2) % 2, chip % 2
    p = y * 2 + (x + y) % 2

    def device(at_z, q):
        at_y = q // 2
        at_x = (q % 2 + at_y) % 2
        return ((at_z * 2 + at_y) * 2 + at_x) * 2 + core

    partner = me + 1 - 2 * core
    after, before, across = (p + 1) % 4, (p + 3) % 4, (p + 2) % 4
    right, left = device(z, after), device(z, before)
    above, below = device((z + 1) % LINE, p), device((z + LINE - 1) % LINE, p)
    not_top, not_bottom = z < LINE - 1, z > 0
    power = (1 + 3 * (z % 2)) * (1 + 15 * (z // 2))

    def order(table, k):
        packed = sum(table[i][k] * LINE**i for i in range(LINE))
        return (packed // power) % LINE

    names = {}

    def flag(name, at=0):
        base = names.setdefault(name, len(names))
        return sem.at[base * 2 * LINE + at]

    pending = []

    def always(body):
        body()

    def send(source, target, name, at, to, condition=None):
        copy = pltpu.make_async_remote_copy(
            src_ref=source, dst_ref=target, send_sem=flag(name + "s", at),
            recv_sem=flag(name + "r", at), device_id={"expert": to}, device_id_type=MESH,
        )
        when = always if condition is None else pl.when(condition)

        @when
        def _():
            copy.start()

        pending.append((when, copy))

    def arrived(target, name, at=0):
        pltpu.make_async_remote_copy(
            src_ref=target, dst_ref=target, send_sem=flag(name + "s", at),
            recv_sem=flag(name + "r", at), device_id={"expert": partner}, device_id_type=MESH,
        ).wait_recv()

    def local(source, target, name):
        copy = pltpu.make_async_copy(source, target, flag(name))
        copy.start()
        return copy

    def span(at_z, q):
        return pl.ds(pl.multiple_of((at_z * RING + q) * block, block), block)

    def part_span(at_z, q, side):
        return pl.ds(pl.multiple_of((at_z * RING + q) * block + side * rows, rows), rows)

    def plane_span(at_z):
        return pl.ds(pl.multiple_of(at_z * plane, plane), plane)

    kept = pl.ds(pl.multiple_of(core * half, half), half)
    given = pl.ds(pl.multiple_of((1 - core) * half, half), half)
    my_rows = part_span(z, p, core)
    its_rows = part_span(z, p, 1 - core)
    front, tail = pl.ds(0, half), pl.ds(half, TAIL)
    core_rows = pl.ds(pl.multiple_of(core * rows, rows), rows)
    other_rows = pl.ds(pl.multiple_of((1 - core) * rows, rows), rows)

    tok_load = local(tokens.at[:, kept], tok.at[my_rows, front], "tok")
    gate_load = local(gate_up.at[0], gate, "gate")
    down_load = local(down_proj.at[0], down, "down")
    taught_load = local(teacher.at[:, kept], taught.at[core_rows, :], "taught")

    barrier = pltpu.get_barrier_semaphore()
    for to in (partner, right, left):
        pl.semaphore_signal(barrier, inc=1, device_id={"expert": to}, device_id_type=MESH)

    @pl.when(not_top)
    def _():
        pl.semaphore_signal(barrier, inc=1, device_id={"expert": above}, device_id_type=MESH)

    @pl.when(not_bottom)
    def _():
        pl.semaphore_signal(barrier, inc=1, device_id={"expert": below}, device_id_type=MESH)

    lane = lax.broadcasted_iota(jnp.int32, (rows, TAIL), 1)
    weight = jnp.zeros((rows, TAIL), jnp.float32)
    named, shares = ids[...].T, combine[...].T
    for k in range(ids.shape[0]):
        match = named[:, k : k + 1] == lax.rem(lane, experts)
        weight += jnp.where(match, shares[:, k : k + 1], 0.0)
    high = weight.astype(jnp.bfloat16).astype(jnp.float32)
    middle = (weight - high).astype(jnp.bfloat16).astype(jnp.float32)
    low = weight - high - middle
    coded = jnp.where(lane < experts, high, jnp.where(lane < 2 * experts, middle, low))
    coded = jnp.where(lane < 3 * experts, coded, 0.0)
    tok[my_rows, tail] = coded.astype(jnp.bfloat16)

    pl.semaphore_wait(barrier, 3 + (LINE - 1 - z + LINE - 2) // (LINE - 1) + (z + LINE - 2) // (LINE - 1))

    send(tokens.at[:, given], tok.at[my_rows, front], "tokx", 0, partner)
    send(tok.at[my_rows, tail], tok.at[my_rows, tail], "tailx", 0, partner)
    send(teacher.at[:, given], taught.at[core_rows, :], "taughtx", 0, partner)

    def start(buffer, tag, k):
        at_z = order(GATHER_ORDER, k)
        first = tag == "t" and k == 0
        for turn, side in enumerate((core, 1 - core) if first else (0, 1)):
            at = at_z * 2 + side
            here = buffer.at[part_span(at_z, p, side)]
            if k > 0:
                arrived(here, tag + "z", at)
            elif first and turn == 0:
                tok_load.wait()
            elif first:
                arrived(tok.at[its_rows, front], "tokx")
                arrived(tok.at[its_rows, tail], "tailx")
            send(here, here, tag + "z", at, above, (at_z <= z) & not_top)
            copy = pltpu.make_async_remote_copy(
                src_ref=here, dst_ref=here, send_sem=flag(tag + "d", at),
                recv_sem=flag(tag + "zr", at), device_id={"expert": below}, device_id_type=MESH,
            )
            when = pl.when((at_z >= z) & not_bottom)

            @when
            def _(copy=copy):
                copy.start()

            pending.append((when, copy))
            send(here, here, tag + "l", at, right)
            send(here, here, tag + "r", at, left)

    def forward(buffer, tag, k):
        at_z = order(GATHER_ORDER, k)
        piece = buffer.at[part_span(at_z, before, 0)]
        arrived(piece, tag + "l", at_z * 2)
        send(piece, piece, tag + "ol", at_z, right)
        piece = buffer.at[part_span(at_z, after, 1)]
        arrived(piece, tag + "r", at_z * 2 + 1)
        send(piece, piece, tag + "or", at_z, left)

    def complete(buffer, tag, k):
        at_z = order(GATHER_ORDER, k)
        arrived(buffer.at[part_span(at_z, before, 1)], tag + "l", at_z * 2 + 1)
        arrived(buffer.at[part_span(at_z, after, 0)], tag + "r", at_z * 2)
        arrived(buffer.at[part_span(at_z, across, 0)], tag + "ol", at_z)
        arrived(buffer.at[part_span(at_z, across, 1)], tag + "or", at_z)

    def gathered(buffer, tag, visit):
        start(buffer, tag, 0)
        start(buffer, tag, 1)
        forward(buffer, tag, 0)
        start(buffer, tag, 2)
        forward(buffer, tag, 1)
        complete(buffer, tag, 0)
        visit(0)
        start(buffer, tag, 3)
        forward(buffer, tag, 2)
        complete(buffer, tag, 1)
        visit(1)
        forward(buffer, tag, 3)
        complete(buffer, tag, 2)
        visit(2)
        complete(buffer, tag, 3)
        visit(3)

    def multiply(k):
        at_z = order(GATHER_ORDER, k)
        own_pre[k] = jnp.dot(
            tok[plane_span(at_z), front], gate[...], preferred_element_type=jnp.float32
        )
        send(own_pre.at[k], got_pre.at[k], "pre", k, partner)

    def finish(k):
        at_z = order(GATHER_ORDER, k)
        arrived(got_pre.at[k], "pre", k)
        pre = own_pre[k] + got_pre[k]
        gated, up = pre[:, :unit_count], pre[:, unit_count:]
        lanes = lax.broadcasted_iota(jnp.int32, (plane, TAIL), 1)
        mine = (lax.rem(lanes, experts) == chip) & (lanes < 3 * experts)
        coded = tok[plane_span(at_z), tail].astype(jnp.float32)
        share = jnp.sum(jnp.where(mine, coded, 0.0), axis=1, keepdims=True)
        hidden = gated / (1.0 + jnp.exp(-gated)) * up * share
        hidden_t[at_z] = hidden.T.astype(jnp.bfloat16)
        lowered = hidden.astype(jnp.bfloat16)

        @pl.loop(0, half // TILE)
        def _(t):
            columns = pl.ds(pl.multiple_of(t * TILE, TILE), TILE)
            part[plane_span(at_z), columns] = jnp.dot(
                lowered, down[:, columns], preferred_element_type=jnp.float32
            ).astype(jnp.bfloat16)

    def send_first(k):
        at_z = order(REDUCE_ORDER, k)
        send(part.at[part_span(at_z, across, 0)], part_a.at[at_z], "a", at_z, right)
        send(part.at[part_span(at_z, across, 1)], part_b.at[at_z], "b", at_z, left)
        send(part.at[part_span(at_z, after, 1)], part_l.at[at_z, 1], "l1", at_z, right)
        send(part.at[part_span(at_z, before, 0)], part_r.at[at_z, 0], "r0", at_z, left)

    def add_up(target, *terms):
        @pl.loop(0, half // TILE, unroll=4)
        def _(t):
            columns = pl.ds(pl.multiple_of(t * TILE, TILE), TILE)
            value = terms[0](columns).astype(jnp.float32)
            for term in terms[1:]:
                value += term(columns).astype(jnp.float32)
            target(columns, value)

    def send_second(k):
        at_z = order(REDUCE_ORDER, k)
        for name, got, q, side, to in (
            ("a", part_a, after, 0, right), ("b", part_b, before, 1, left)
        ):
            arrived(got.at[at_z], name, at_z)
            piece = part_span(at_z, q, side)

            def put(columns, value, piece=piece):
                part[piece, columns] = value.astype(jnp.bfloat16)

            add_up(put, lambda c, piece=piece: part[piece, c], lambda c, got=got: got[at_z, :, c])
            if side == 0:
                send(part.at[piece], part_l.at[at_z, 0], "l0", at_z, to)
            else:
                send(part.at[piece], part_r.at[at_z, 1], "r1", at_z, to)

    def reduce_line(k):
        for side in range(2):
            reduce_side(k, side)

    def reduce_side(k, side):
        at_z = order(REDUCE_ORDER, k)
        piece = part_span(at_z, p, side)
        inner = pl.ds(side * rows, rows)
        at = at_z * 2 + side
        arrived(part_l.at[at_z, side], "l%d" % side, at_z)
        arrived(part_r.at[at_z, side], "r%d" % side, at_z)

        def put(columns, value):
            rounded = value.astype(jnp.bfloat16)
            if k < LINE - 1:
                part[piece, columns] = rounded
            else:
                student[inner, columns] = rounded
                error = rounded.astype(jnp.float32) - taught[inner, columns].astype(jnp.float32)
                errors[piece, columns] = error.astype(jnp.bfloat16)

        def summed(up, down_too):
            more = []
            if up:
                arrived(line_up.at[at_z, side], "u", at)
                more.append(lambda c: line_up[at_z, side, :, c])
            if down_too:
                arrived(line_down.at[at_z, side], "d", at)
                more.append(lambda c: line_down[at_z, side, :, c])
            add_up(
                put,
                lambda c: part[piece, c],
                lambda c: part_l[at_z, side, :, c],
                lambda c: part_r[at_z, side, :, c],
                *more,
            )

        if k < LINE - 1:
            pl.when((at_z > z) & not_bottom)(lambda: summed(True, False))
            pl.when((at_z < z) & not_top)(lambda: summed(False, True))
            outer = ((at_z > z) & (z == 0)) | ((at_z < z) & (z == LINE - 1))
            pl.when(outer)(lambda: summed(False, False))
            send(part.at[piece], line_up.at[at_z, side], "u", at, above, at_z > z)
            send(part.at[piece], line_down.at[at_z, side], "d", at, below, at_z < z)
        else:
            pl.when(z == 0)(lambda: summed(False, True))
            pl.when(z == LINE - 1)(lambda: summed(True, False))
            pl.when(not_top & not_bottom)(lambda: summed(True, True))

    def forward_visit(k):
        if k == 0:
            gate_load.wait()
        multiply(k)
        if k == 1:
            down_load.wait()
        if k in (1, 2):
            finish(k - 1)
        if k in (2, 3):
            finish(k)
        if k == 2:
            send_first(0)

    gathered(tok, "t", forward_visit)
    send_first(1)
    send_second(0)
    send_first(2)
    send_second(1)
    send_first(3)
    reduce_line(0)
    send_second(2)
    reduce_line(1)
    send_second(3)
    reduce_line(2)
    taught_load.wait()
    arrived(taught.at[other_rows, :], "taughtx")
    reduce_line(3)

    stores = [local(student.at[core_rows, :], student_out.at[:, kept], "student")]

    def backward_visit(k):
        at_z = order(GATHER_ORDER, k)
        if k == 0:
            send(student.at[other_rows, :], student_out.at[:, kept], "studentx", 0, partner)

        @pl.loop(0, half // TILE)
        def _(t):
            columns = pl.ds(pl.multiple_of(t * TILE, TILE), TILE)
            value = jnp.dot(
                hidden_t[at_z], errors[plane_span(at_z), columns], preferred_element_type=jnp.float32
            )
            if k > 0:
                value += total[:, columns]
            if k < LINE - 1:
                total[:, columns] = value
            else:
                grad[:, columns] = value.astype(jnp.bfloat16)

    gathered(errors, "e", backward_visit)
    stores.append(local(grad, grad_out.at[0], "grad"))
    for copy in stores:
        copy.wait()
    arrived(student_out.at[:, given], "studentx")
    for when, copy in pending:
        @when
        def _(copy=copy):
            copy.wait_send()


def fused(tokens, gate_up, down_proj, expert_ids, combine, teacher):
    rows, width = tokens.shape
    half = width // 2
    unit_count = down_proj.shape[1]
    all_rows, block = RING * LINE * 2 * rows, 2 * rows
    plane = RING * block
    anywhere, vmem = pl.BlockSpec(memory_space=pl.ANY), pl.BlockSpec(memory_space=pltpu.VMEM)
    low, full = jnp.bfloat16, jnp.float32
    return pl.pallas_call(
        kernel,
        out_shape=(
            jax.ShapeDtypeStruct((rows, width), low),
            jax.ShapeDtypeStruct((1, unit_count, half), low),
        ),
        in_specs=[anywhere, anywhere, anywhere, vmem, vmem, anywhere],
        out_specs=(anywhere, anywhere),
        scratch_shapes=[
            pltpu.VMEM((all_rows, half + TAIL), low),
            pltpu.VMEM((half, 2 * unit_count), low),
            pltpu.VMEM((unit_count, half), low),
            pltpu.VMEM((block, half), low),
            pltpu.VMEM((LINE, plane, 2 * unit_count), full),
            pltpu.VMEM((LINE, plane, 2 * unit_count), full),
            pltpu.VMEM((LINE, unit_count, plane), low),
            pltpu.VMEM((all_rows, half), low),
            pltpu.VMEM((LINE, rows, half), low),
            pltpu.VMEM((LINE, rows, half), low),
            pltpu.VMEM((LINE, 2, rows, half), low),
            pltpu.VMEM((LINE, 2, rows, half), low),
            pltpu.VMEM((LINE, 2, rows, half), low),
            pltpu.VMEM((LINE, 2, rows, half), low),
            pltpu.VMEM((block, half), low),
            pltpu.VMEM((all_rows, half), low),
            pltpu.VMEM((unit_count, half), full),
            pltpu.VMEM((unit_count, half), low),
            pltpu.SemaphoreType.DMA((120 * LINE,)),
        ],
        compiler_params=pltpu.CompilerParams(
            collective_id=0, has_side_effects=True, vmem_limit_bytes=56 * 2**20
        ),
        cost_estimate=pl.CostEstimate(flops=5 * 10**9, bytes_accessed=10**7, transcendentals=10**5),
    )(tokens, gate_up, down_proj, expert_ids.T, combine.T, teacher)


def swap_cores(block):
    count = lax.axis_size("expert")
    return lax.ppermute(block, "expert", [(i, i ^ 1) for i in range(count)])


def dense_weights(expert_ids, combine, experts):
    match = expert_ids[:, :, None] == jnp.arange(experts, dtype=jnp.int32)[None, None, :]
    return jnp.sum(jnp.where(match, combine[:, :, None], 0.0), axis=1)


def spread(tokens, gate_up, down_proj, expert_ids, combine, teacher):
    row_count, width = tokens.shape
    count = lax.axis_size("expert")
    experts = count // 2
    unit_count = down_proj.shape[1]
    half = width // 2
    me = lax.axis_index("expert")
    expert, core = me // 2, me % 2
    same_core = [list(range(0, count, 2)), list(range(1, count, 2))]

    def chip_rows(rows):
        kept = lax.dynamic_slice(rows, (0, core * half), (row_count, half))
        given = lax.dynamic_slice(rows, (0, (1 - core) * half), (row_count, half))
        got = swap_cores(given)
        first = jnp.where(core == 0, kept, got)
        second = jnp.where(core == 0, got, kept)
        return jnp.concatenate([first, second], axis=0)

    def gather(block):
        return lax.all_gather(block, "expert", axis_index_groups=same_core, axis=0, tiled=True)

    weights = lax.all_gather(dense_weights(expert_ids, combine, experts), "expert", axis=0, tiled=True)
    weight = lax.dynamic_slice(weights, (0, expert), (weights.shape[0], 1))
    taught = chip_rows(teacher)
    rows_in = gather(chip_rows(tokens))
    partial = jnp.dot(rows_in, gate_up[0], preferred_element_type=jnp.float32)
    pre = partial + swap_cores(partial)
    hidden = jax.nn.silu(pre[:, :unit_count]) * pre[:, unit_count:]
    weighed = (weight * hidden).astype(jnp.bfloat16)
    part = jnp.dot(weighed, down_proj[0], preferred_element_type=jnp.float32).astype(jnp.bfloat16)
    block = lax.psum_scatter(part, "expert", axis_index_groups=same_core, scatter_dimension=0, tiled=True)
    error = (block.astype(jnp.float32) - taught.astype(jnp.float32)).astype(jnp.bfloat16)
    mine = lax.dynamic_slice(block, (core * row_count, 0), (row_count, half))
    theirs = swap_cores(lax.dynamic_slice(block, ((1 - core) * row_count, 0), (row_count, half)))
    student = jnp.concatenate(
        [jnp.where(core == 0, mine, theirs), jnp.where(core == 0, theirs, mine)], axis=1
    )
    errors = gather(error)
    gradient = jnp.einsum("su,sd->ud", weighed, errors, preferred_element_type=jnp.float32)
    return (student, gradient.astype(jnp.bfloat16).reshape(1, unit_count, half))


def solution(mesh):
    in_specs = (
        P(("groups", "expert"), None),
        P(("groups", "expert"), None, None),
        P(("groups", "expert"), None, None),
        P(("groups", "expert"), None),
        P(("groups", "expert"), None),
        P(("groups", "expert"), None),
    )
    out_specs = (P(("groups", "expert"), None), P(("groups", "expert"), None, None))
    small = mesh.shape["expert"] == 2 * RING * LINE
    shards = fused if small else spread
    return jax.shard_map(shards, mesh=mesh, in_specs=in_specs, out_specs=out_specs, check_vma=False)
```

```python
import functools

import jax
import jax.numpy as jnp
from jax import lax
from jax.experimental import pallas as pl
from jax.experimental.pallas import tpu as pltpu
from jax.sharding import PartitionSpec as P

MESH = pl.DeviceIdType.MESH
RING, LINE, TAIL, TILE = 4, 4, 128, 512
GATHER_ORDER = ((0, 1, 2, 3), (1, 2, 0, 3), (2, 1, 3, 0), (3, 2, 1, 0))
REDUCE_ORDER = ((2, 3, 1, 0), (2, 3, 0, 1), (1, 0, 3, 2), (1, 0, 2, 3))


def kernel(
    tokens, gate_up, down_proj, ids, combine, teacher, student_out, grad_out,
    tok, gate, down, taught, own_pre, got_pre, hidden_t, part, part_a, part_b,
    part_l, part_r, line_up, line_down, student, errors, total, grad, sem,
):
    rows = tokens.shape[0]
    block, plane = 2 * rows, RING * 2 * rows
    half = down.shape[1]
    unit_count = down.shape[0]
    experts = RING * LINE
    me = lax.axis_index("expert")
    core, chip = me % 2, me // 2
    z, y, x = chip // 4, (chip // 2) % 2, chip % 2
    p = y * 2 + (x + y) % 2

    def device(at_z, q):
        at_y = q // 2
        at_x = (q % 2 + at_y) % 2
        return ((at_z * 2 + at_y) * 2 + at_x) * 2 + core

    partner = me + 1 - 2 * core
    after, before, across = (p + 1) % 4, (p + 3) % 4, (p + 2) % 4
    right, left = device(z, after), device(z, before)
    above, below = device((z + 1) % LINE, p), device((z + LINE - 1) % LINE, p)
    not_top, not_bottom = z < LINE - 1, z > 0
    power = (1 + 3 * (z % 2)) * (1 + 15 * (z // 2))

    def order(table, k):
        packed = sum(table[i][k] * LINE**i for i in range(LINE))
        return (packed // power) % LINE

    names = {}

    def flag(name, at=0):
        base = names.setdefault(name, len(names))
        return sem.at[base * 2 * LINE + at]

    pending = []

    def always(body):
        body()

    def send(source, target, name, at, to, condition=None):
        copy = pltpu.make_async_remote_copy(
            src_ref=source, dst_ref=target, send_sem=flag(name + "s", at),
            recv_sem=flag(name + "r", at), device_id={"expert": to}, device_id_type=MESH,
        )
        when = always if condition is None else pl.when(condition)

        @when
        def _():
            copy.start()

        pending.append((when, copy))

    def arrived(target, name, at=0):
        pltpu.make_async_remote_copy(
            src_ref=target, dst_ref=target, send_sem=flag(name + "s", at),
            recv_sem=flag(name + "r", at), device_id={"expert": partner}, device_id_type=MESH,
        ).wait_recv()

    def local(source, target, name):
        copy = pltpu.make_async_copy(source, target, flag(name))
        copy.start()
        return copy

    def span(at_z, q):
        return pl.ds(pl.multiple_of((at_z * RING + q) * block, block), block)

    def part_span(at_z, q, side):
        return pl.ds(pl.multiple_of((at_z * RING + q) * block + side * rows, rows), rows)

    def plane_span(at_z):
        return pl.ds(pl.multiple_of(at_z * plane, plane), plane)

    kept = pl.ds(pl.multiple_of(core * half, half), half)
    given = pl.ds(pl.multiple_of((1 - core) * half, half), half)
    my_rows = part_span(z, p, core)
    its_rows = part_span(z, p, 1 - core)
    front, tail = pl.ds(0, half), pl.ds(half, TAIL)
    core_rows = pl.ds(pl.multiple_of(core * rows, rows), rows)
    other_rows = pl.ds(pl.multiple_of((1 - core) * rows, rows), rows)

    tok_load = local(tokens.at[:, kept], tok.at[my_rows, front], "tok")
    gate_load = local(gate_up.at[0], gate, "gate")
    down_load = local(down_proj.at[0], down, "down")
    taught_load = local(teacher.at[:, kept], taught.at[core_rows, :], "taught")

    barrier = pltpu.get_barrier_semaphore()
    for to in (partner, right, left):
        pl.semaphore_signal(barrier, inc=1, device_id={"expert": to}, device_id_type=MESH)

    @pl.when(not_top)
    def _():
        pl.semaphore_signal(barrier, inc=1, device_id={"expert": above}, device_id_type=MESH)

    @pl.when(not_bottom)
    def _():
        pl.semaphore_signal(barrier, inc=1, device_id={"expert": below}, device_id_type=MESH)

    lane = lax.broadcasted_iota(jnp.int32, (rows, TAIL), 1)
    weight = jnp.zeros((rows, TAIL), jnp.float32)
    named, shares = ids[...].T, combine[...].T
    for k in range(ids.shape[0]):
        match = named[:, k : k + 1] == lax.rem(lane, experts)
        weight += jnp.where(match, shares[:, k : k + 1], 0.0)
    high = weight.astype(jnp.bfloat16).astype(jnp.float32)
    middle = (weight - high).astype(jnp.bfloat16).astype(jnp.float32)
    low = weight - high - middle
    coded = jnp.where(lane < experts, high, jnp.where(lane < 2 * experts, middle, low))
    coded = jnp.where(lane < 3 * experts, coded, 0.0)
    tok[my_rows, tail] = coded.astype(jnp.bfloat16)

    pl.semaphore_wait(barrier, 3 + (LINE - 1 - z + LINE - 2) // (LINE - 1) + (z + LINE - 2) // (LINE - 1))

    send(tokens.at[:, given], tok.at[my_rows, front], "tokx", 0, partner)
    send(tok.at[my_rows, tail], tok.at[my_rows, tail], "tailx", 0, partner)
    send(teacher.at[:, given], taught.at[core_rows, :], "taughtx", 0, partner)

    def start(buffer, tag, k):
        at_z = order(GATHER_ORDER, k)
        first = tag == "t" and k == 0
        for turn, side in enumerate((core, 1 - core) if first else (0, 1)):
            at = at_z * 2 + side
            here = buffer.at[part_span(at_z, p, side)]
            if k > 0:
                arrived(here, tag + "z", at)
            elif first and turn == 0:
                tok_load.wait()
            elif first:
                arrived(tok.at[its_rows, front], "tokx")
                arrived(tok.at[its_rows, tail], "tailx")
            send(here, here, tag + "z", at, above, (at_z <= z) & not_top)
            copy = pltpu.make_async_remote_copy(
                src_ref=here, dst_ref=here, send_sem=flag(tag + "d", at),
                recv_sem=flag(tag + "zr", at), device_id={"expert": below}, device_id_type=MESH,
            )
            when = pl.when((at_z >= z) & not_bottom)

            @when
            def _(copy=copy):
                copy.start()

            pending.append((when, copy))
            send(here, here, tag + "l", at, right)
            send(here, here, tag + "r", at, left)

    def forward(buffer, tag, k):
        at_z = order(GATHER_ORDER, k)
        piece = buffer.at[part_span(at_z, before, 0)]
        arrived(piece, tag + "l", at_z * 2)
        send(piece, piece, tag + "ol", at_z, right)
        piece = buffer.at[part_span(at_z, after, 1)]
        arrived(piece, tag + "r", at_z * 2 + 1)
        send(piece, piece, tag + "or", at_z, left)

    def complete(buffer, tag, k):
        at_z = order(GATHER_ORDER, k)
        arrived(buffer.at[part_span(at_z, before, 1)], tag + "l", at_z * 2 + 1)
        arrived(buffer.at[part_span(at_z, after, 0)], tag + "r", at_z * 2)
        arrived(buffer.at[part_span(at_z, across, 0)], tag + "ol", at_z)
        arrived(buffer.at[part_span(at_z, across, 1)], tag + "or", at_z)

    def gathered(buffer, tag, visit):
        start(buffer, tag, 0)
        start(buffer, tag, 1)
        forward(buffer, tag, 0)
        start(buffer, tag, 2)
        forward(buffer, tag, 1)
        start(buffer, tag, 3)
        forward(buffer, tag, 2)
        complete(buffer, tag, 0)
        visit(0)
        complete(buffer, tag, 1)
        visit(1)
        forward(buffer, tag, 3)
        complete(buffer, tag, 2)
        visit(2)
        complete(buffer, tag, 3)
        visit(3)

    def multiply(k):
        at_z = order(GATHER_ORDER, k)
        own_pre[k] = jnp.dot(
            tok[plane_span(at_z), front], gate[...], preferred_element_type=jnp.float32
        )
        send(own_pre.at[k], got_pre.at[k], "pre", k, partner)

    def finish(k):
        at_z = order(GATHER_ORDER, k)
        arrived(got_pre.at[k], "pre", k)
        pre = own_pre[k] + got_pre[k]
        gated, up = pre[:, :unit_count], pre[:, unit_count:]
        lanes = lax.broadcasted_iota(jnp.int32, (plane, TAIL), 1)
        mine = (lax.rem(lanes, experts) == chip) & (lanes < 3 * experts)
        coded = tok[plane_span(at_z), tail].astype(jnp.float32)
        share = jnp.sum(jnp.where(mine, coded, 0.0), axis=1, keepdims=True)
        hidden = gated / (1.0 + jnp.exp(-gated)) * up * share
        hidden_t[at_z] = hidden.T.astype(jnp.bfloat16)
        lowered = hidden.astype(jnp.bfloat16)

        @pl.loop(0, half // TILE)
        def _(t):
            columns = pl.ds(pl.multiple_of(t * TILE, TILE), TILE)
            part[plane_span(at_z), columns] = jnp.dot(
                lowered, down[:, columns], preferred_element_type=jnp.float32
            ).astype(jnp.bfloat16)

    def send_first(k):
        at_z = order(REDUCE_ORDER, k)
        send(part.at[part_span(at_z, across, 0)], part_a.at[at_z], "a", at_z, right)
        send(part.at[part_span(at_z, across, 1)], part_b.at[at_z], "b", at_z, left)
        send(part.at[part_span(at_z, after, 1)], part_l.at[at_z, 1], "l1", at_z, right)
        send(part.at[part_span(at_z, before, 0)], part_r.at[at_z, 0], "r0", at_z, left)

    def add_up(target, *terms):
        @pl.loop(0, half // TILE, unroll=4)
        def _(t):
            columns = pl.ds(pl.multiple_of(t * TILE, TILE), TILE)
            value = terms[0](columns).astype(jnp.float32)
            for term in terms[1:]:
                value += term(columns).astype(jnp.float32)
            target(columns, value)

    def send_second(k):
        at_z = order(REDUCE_ORDER, k)
        for name, got, q, side, to in (
            ("a", part_a, after, 0, right), ("b", part_b, before, 1, left)
        ):
            arrived(got.at[at_z], name, at_z)
            piece = part_span(at_z, q, side)

            def put(columns, value, piece=piece):
                part[piece, columns] = value.astype(jnp.bfloat16)

            add_up(put, lambda c, piece=piece: part[piece, c], lambda c, got=got: got[at_z, :, c])
            if side == 0:
                send(part.at[piece], part_l.at[at_z, 0], "l0", at_z, to)
            else:
                send(part.at[piece], part_r.at[at_z, 1], "r1", at_z, to)

    def reduce_line(k):
        for side in range(2):
            reduce_side(k, side)

    def reduce_side(k, side):
        at_z = order(REDUCE_ORDER, k)
        piece = part_span(at_z, p, side)
        inner = pl.ds(side * rows, rows)
        at = at_z * 2 + side
        arrived(part_l.at[at_z, side], "l%d" % side, at_z)
        arrived(part_r.at[at_z, side], "r%d" % side, at_z)

        def put(columns, value):
            rounded = value.astype(jnp.bfloat16)
            if k < LINE - 1:
                part[piece, columns] = rounded
            else:
                student[inner, columns] = rounded
                error = rounded.astype(jnp.float32) - taught[inner, columns].astype(jnp.float32)
                errors[piece, columns] = error.astype(jnp.bfloat16)

        def summed(up, down_too):
            more = []
            if up:
                arrived(line_up.at[at_z, side], "u", at)
                more.append(lambda c: line_up[at_z, side, :, c])
            if down_too:
                arrived(line_down.at[at_z, side], "d", at)
                more.append(lambda c: line_down[at_z, side, :, c])
            add_up(
                put,
                lambda c: part[piece, c],
                lambda c: part_l[at_z, side, :, c],
                lambda c: part_r[at_z, side, :, c],
                *more,
            )

        if k < LINE - 1:
            pl.when((at_z > z) & not_bottom)(lambda: summed(True, False))
            pl.when((at_z < z) & not_top)(lambda: summed(False, True))
            outer = ((at_z > z) & (z == 0)) | ((at_z < z) & (z == LINE - 1))
            pl.when(outer)(lambda: summed(False, False))
            send(part.at[piece], line_up.at[at_z, side], "u", at, above, at_z > z)
            send(part.at[piece], line_down.at[at_z, side], "d", at, below, at_z < z)
        else:
            pl.when(z == 0)(lambda: summed(False, True))
            pl.when(z == LINE - 1)(lambda: summed(True, False))
            pl.when(not_top & not_bottom)(lambda: summed(True, True))

    def forward_visit(k):
        if k == 0:
            gate_load.wait()
        multiply(k)
        if k == 1:
            down_load.wait()
        if k in (1, 2):
            finish(k - 1)
        if k in (2, 3):
            finish(k)
        if k == 2:
            send_first(0)

    gathered(tok, "t", forward_visit)
    send_first(1)
    send_second(0)
    send_first(2)
    send_second(1)
    send_first(3)
    reduce_line(0)
    send_second(2)
    reduce_line(1)
    send_second(3)
    reduce_line(2)
    taught_load.wait()
    arrived(taught.at[other_rows, :], "taughtx")
    reduce_line(3)

    stores = [local(student.at[core_rows, :], student_out.at[:, kept], "student")]

    def backward_visit(k):
        at_z = order(GATHER_ORDER, k)
        if k == 0:
            send(student.at[other_rows, :], student_out.at[:, kept], "studentx", 0, partner)

        @pl.loop(0, half // TILE)
        def _(t):
            columns = pl.ds(pl.multiple_of(t * TILE, TILE), TILE)
            value = jnp.dot(
                hidden_t[at_z], errors[plane_span(at_z), columns], preferred_element_type=jnp.float32
            )
            if k > 0:
                value += total[:, columns]
            if k < LINE - 1:
                total[:, columns] = value
            else:
                grad[:, columns] = value.astype(jnp.bfloat16)
                pltpu.make_async_copy(
                    grad.at[:, columns], grad_out.at[0, :, columns], flag("grad")
                ).start()

    gathered(errors, "e", backward_visit)
    stores.append(pltpu.make_async_copy(grad, grad_out.at[0], flag("grad")))
    for copy in stores:
        copy.wait()
    arrived(student_out.at[:, given], "studentx")
    for when, copy in pending:
        @when
        def _(copy=copy):
            copy.wait_send()


def fused(tokens, gate_up, down_proj, expert_ids, combine, teacher):
    rows, width = tokens.shape
    half = width // 2
    unit_count = down_proj.shape[1]
    all_rows, block = RING * LINE * 2 * rows, 2 * rows
    plane = RING * block
    anywhere, vmem = pl.BlockSpec(memory_space=pl.ANY), pl.BlockSpec(memory_space=pltpu.VMEM)
    low, full = jnp.bfloat16, jnp.float32
    return pl.pallas_call(
        kernel,
        out_shape=(
            jax.ShapeDtypeStruct((rows, width), low),
            jax.ShapeDtypeStruct((1, unit_count, half), low),
        ),
        in_specs=[anywhere, anywhere, anywhere, vmem, vmem, anywhere],
        out_specs=(anywhere, anywhere),
        scratch_shapes=[
            pltpu.VMEM((all_rows, half + TAIL), low),
            pltpu.VMEM((half, 2 * unit_count), low),
            pltpu.VMEM((unit_count, half), low),
            pltpu.VMEM((block, half), low),
            pltpu.VMEM((LINE, plane, 2 * unit_count), full),
            pltpu.VMEM((LINE, plane, 2 * unit_count), full),
            pltpu.VMEM((LINE, unit_count, plane), low),
            pltpu.VMEM((all_rows, half), low),
            pltpu.VMEM((LINE, rows, half), low),
            pltpu.VMEM((LINE, rows, half), low),
            pltpu.VMEM((LINE, 2, rows, half), low),
            pltpu.VMEM((LINE, 2, rows, half), low),
            pltpu.VMEM((LINE, 2, rows, half), low),
            pltpu.VMEM((LINE, 2, rows, half), low),
            pltpu.VMEM((block, half), low),
            pltpu.VMEM((all_rows, half), low),
            pltpu.VMEM((unit_count, half), full),
            pltpu.VMEM((unit_count, half), low),
            pltpu.SemaphoreType.DMA((120 * LINE,)),
        ],
        compiler_params=pltpu.CompilerParams(
            collective_id=0, has_side_effects=True, vmem_limit_bytes=56 * 2**20
        ),
        cost_estimate=pl.CostEstimate(flops=5 * 10**9, bytes_accessed=10**7, transcendentals=10**5),
    )(tokens, gate_up, down_proj, expert_ids.T, combine.T, teacher)


def swap_cores(block):
    count = lax.axis_size("expert")
    return lax.ppermute(block, "expert", [(i, i ^ 1) for i in range(count)])


def dense_weights(expert_ids, combine, experts):
    match = expert_ids[:, :, None] == jnp.arange(experts, dtype=jnp.int32)[None, None, :]
    return jnp.sum(jnp.where(match, combine[:, :, None], 0.0), axis=1)


def spread(tokens, gate_up, down_proj, expert_ids, combine, teacher):
    row_count, width = tokens.shape
    count = lax.axis_size("expert")
    experts = count // 2
    unit_count = down_proj.shape[1]
    half = width // 2
    me = lax.axis_index("expert")
    expert, core = me // 2, me % 2
    same_core = [list(range(0, count, 2)), list(range(1, count, 2))]

    def chip_rows(rows):
        kept = lax.dynamic_slice(rows, (0, core * half), (row_count, half))
        given = lax.dynamic_slice(rows, (0, (1 - core) * half), (row_count, half))
        got = swap_cores(given)
        first = jnp.where(core == 0, kept, got)
        second = jnp.where(core == 0, got, kept)
        return jnp.concatenate([first, second], axis=0)

    def gather(block):
        return lax.all_gather(block, "expert", axis_index_groups=same_core, axis=0, tiled=True)

    weights = lax.all_gather(dense_weights(expert_ids, combine, experts), "expert", axis=0, tiled=True)
    weight = lax.dynamic_slice(weights, (0, expert), (weights.shape[0], 1))
    taught = chip_rows(teacher)
    rows_in = gather(chip_rows(tokens))
    partial = jnp.dot(rows_in, gate_up[0], preferred_element_type=jnp.float32)
    pre = partial + swap_cores(partial)
    hidden = jax.nn.silu(pre[:, :unit_count]) * pre[:, unit_count:]
    weighed = (weight * hidden).astype(jnp.bfloat16)
    part = jnp.dot(weighed, down_proj[0], preferred_element_type=jnp.float32).astype(jnp.bfloat16)
    block = lax.psum_scatter(part, "expert", axis_index_groups=same_core, scatter_dimension=0, tiled=True)
    error = (block.astype(jnp.float32) - taught.astype(jnp.float32)).astype(jnp.bfloat16)
    mine = lax.dynamic_slice(block, (core * row_count, 0), (row_count, half))
    theirs = swap_cores(lax.dynamic_slice(block, ((1 - core) * row_count, 0), (row_count, half)))
    student = jnp.concatenate(
        [jnp.where(core == 0, mine, theirs), jnp.where(core == 0, theirs, mine)], axis=1
    )
    errors = gather(error)
    gradient = jnp.einsum("su,sd->ud", weighed, errors, preferred_element_type=jnp.float32)
    return (student, gradient.astype(jnp.bfloat16).reshape(1, unit_count, half))


def solution(mesh):
    in_specs = (
        P(("groups", "expert"), None),
        P(("groups", "expert"), None, None),
        P(("groups", "expert"), None, None),
        P(("groups", "expert"), None),
        P(("groups", "expert"), None),
        P(("groups", "expert"), None),
    )
    out_specs = (P(("groups", "expert"), None), P(("groups", "expert"), None, None))
    small = mesh.shape["expert"] == 2 * RING * LINE
    shards = fused if small else spread
    return jax.shard_map(shards, mesh=mesh, in_specs=in_specs, out_specs=out_specs, check_vma=False)
```
